256 devices in a mesh: dp: 256 (over x, z, y, core).
Axes of the slice: x: 4, y: 4, z: 8, core: 2. Of those that a mesh axis runs over, the one named last changes fastest.
Arguments:
- image_embeds: bfloat16 [131072, 1152], P('dp'), may hold values from -6 to 6
- text_embeds: bfloat16 [131072, 1152], P('dp'), may hold values from -6 to 6
- logit_scale: float32 [1], replicated, may hold values from 0.02 to 0.06
- logit_bias: float32 [1], replicated, may hold values from -4 to -1
- plan: int32 [256, 6], P('dp'), may hold values from 0 to 255, as said below
Outputs:
- image_grad: float32 [131072, 1152], P('dp')
- text_grad: float32 [131072, 1152], P('dp')
- loss_tiles: float32 [256, 7], P('dp')
The draws below stay inside these ranges and needn't reach their ends.
Inputs may be any that keep to these rules, and one draw needn't show every extreme that they name: In round r every block d meets plan[d, r] = d XOR (m_r * 32), where the round mask m_r lies in 1 to 7 and is the same for every d; the 6 masks differ from one another.
All inputs are finite; a program needn't handle non-finite values.
Results may differ from the reference program's by a relative error of at most 0.0028.
Values may be sent and summed in bfloat16 or wider, within the bound.
No kernel may reach another device: no remote copies, remote signals or barrier semaphores. Data moves between devices by JAX's collectives and lax.ppermute only.
A program may use at most 128 MiB of HBM per device.

```python
import math
import jax
import jax.numpy as jnp

D = 1152
ROUNDS = 6
GROUP = 8
PLAYERS = 256
STRIDE = 32
PAIRS = 131072


def draw_plan(key, part):
    key = jax.random.fold_in(key, 11)
    round_masks = jax.random.permutation(key, GROUP - 1)[:ROUNDS].astype(jnp.int32) + 1
    player_ids = jnp.arange(PLAYERS, dtype=jnp.int32)
    return jnp.bitwise_xor(player_ids[:, None], (round_masks * STRIDE).astype(jnp.int32)[None, :]).astype(jnp.int32)


def level_of(own_key, dims, cuts, low, high):
    loudness = 1.0
    for axis_at, shards_of in cuts:
        steps = jax.random.uniform(jax.random.fold_in(jax.random.fold_in(own_key, 6), axis_at), (shards_of,), jnp.float32, low / len(cuts), high / len(cuts))
        loudness = loudness * jnp.repeat(jnp.exp(steps), dims[axis_at] // shards_of).reshape((-1,) + (1,) * (len(dims) - 1 - axis_at))
    return loudness


def scatter_about(key, dims, deviation, limit, cuts=(), kind=jnp.bfloat16):
    entries = jax.random.normal(key, dims, jnp.float32) * deviation
    if len(cuts) > 0:
        entries = level_of(key, dims, cuts, -0.22, 0.18) * entries
    return jnp.clip(entries, min=-limit, max=limit).astype(kind)


def setup_inputs(seed: int = 0) -> dict:
    arg_keys = jax.random.split(jax.random.key(seed), 6)
    return {
        "image_embeds": scatter_about(arg_keys[0], (PAIRS, D), 1.0, 6.0, ((0, 256),)),
        "text_embeds": scatter_about(arg_keys[1], (PAIRS, D), 1.0, 6.0, ((0, 256),)),
        "logit_scale": jnp.clip(jnp.exp(jax.random.uniform(arg_keys[2], (1,), jnp.float32, math.log(0.02), math.log(0.06))), 0.02, 0.06),
        "logit_bias": jnp.clip(jax.random.uniform(arg_keys[3], (1,), jnp.float32, -4.0, -1.0), -4.0, -1.0),
        "plan": draw_plan(jax.random.fold_in(arg_keys[5], 71), 0),
    }


def pair_tile(images, partner, logit_mult, logit_shift, label_sign):
    image_wide = images.astype(jnp.float32)
    partner_wide = partner.astype(jnp.float32)
    scores = jnp.einsum("nid,njd->nij", image_wide, partner_wide)
    logits = logit_mult * scores + logit_shift
    tile_loss = jnp.mean(jax.nn.softplus(-label_sign * logits), axis=(1, 2))
    coefficient = (-label_sign * jax.nn.sigmoid(-label_sign * logits) * logit_mult).astype(jnp.bfloat16)
    coefficient_wide = coefficient.astype(jnp.float32)
    image_part = jnp.einsum("nij,njd->nid", coefficient_wide, partner_wide)
    text_part = jnp.einsum("nij,nid->njd", coefficient_wide, image_wide).astype(jnp.bfloat16)
    return tile_loss, image_part, text_part


def reference(image_embeds, text_embeds, logit_scale, logit_bias, plan):
    player_count = plan.shape[0]
    round_count = plan.shape[1]
    width = image_embeds.shape[1]
    pair_rows = image_embeds.shape[0] // player_count
    images = image_embeds.reshape(player_count, pair_rows, width)
    text_blocks = text_embeds.reshape(player_count, pair_rows, width)
    logit_mult = logit_scale[0]
    logit_shift = logit_bias[0]
    diagonal_mask = jnp.eye(pair_rows, dtype=bool)
    home_sign = jnp.where(diagonal_mask, 1.0, -1.0).astype(jnp.float32)
    away_sign = jnp.full((pair_rows, pair_rows), -1.0, jnp.float32)
    home_loss, image_grad, home_text = pair_tile(images, text_blocks, logit_mult, logit_shift, home_sign)
    text_grad = home_text.astype(jnp.float32)
    tile_losses = [home_loss]
    for round_no in range(round_count):
        partner = plan[:, round_no].astype(jnp.int32)
        tile_loss, image_part, text_part = pair_tile(images, text_blocks[partner], logit_mult, logit_shift, away_sign)
        image_grad = image_grad + image_part
        text_grad = text_grad + text_part[partner].astype(jnp.float32)
        tile_losses.append(tile_loss)
    return (image_grad.reshape(player_count * pair_rows, width),
            text_grad.reshape(player_count * pair_rows, width),
            jnp.stack(tile_losses, axis=1))
```

```python
import functools

import jax
import jax.numpy as jnp
from jax import lax
from jax.experimental import pallas as pl
from jax.experimental.pallas import tpu as pltpu
from jax.sharding import PartitionSpec as P

X_SHIFT = 6
Z_BIT = 5
SUB = 256
VMEM_BYTES = 28 << 20


def x_neighbour(index, hop):
    x = index >> X_SHIFT
    return (index & ((1 << X_SHIFT) - 1)) | (((x + hop) & 3) << X_SHIFT)


def to_x(value, hop):
    count = lax.axis_size("dp")
    return lax.ppermute(value, "dp", [(i, x_neighbour(i, hop)) for i in range(count)])


def to_z(value):
    count = lax.axis_size("dp")
    return lax.ppermute(value, "dp", [(i, i ^ (1 << Z_BIT)) for i in range(count)])


def softplus_and_slope(u):
    decay = jnp.exp(-jnp.abs(u))
    ratio = 1.0 / (1.0 + decay)
    slope = jnp.where(u >= 0.0, ratio, decay * ratio)
    return jnp.maximum(u, 0.0) + jnp.log1p(decay), slope


def tiles_kernel(blocks, home, add_to, scalars, flags, images, *rest):
    texts = rest[:blocks]
    rest = rest[blocks:]
    if add_to:
        earlier, rest = rest[0], rest[1:]
    coefs = rest[:blocks]
    grad, losses, scores, total = rest[blocks:]
    rows, width = images.shape
    scale, shift = scalars[0], scalars[1]
    units = [(i, k) for i in range(blocks) for k in range(0, texts[i].shape[0], SUB)]

    def score(unit):
        i, k = unit
        return lax.dot_general(
            texts[i][k : k + SUB, :],
            images[...],
            (((1,), (1,)), ((), ())),
            preferred_element_type=jnp.float32,
        )

    sums = [jnp.zeros((8, rows), jnp.float32) for _ in range(blocks)]
    scores[0] = score(units[0])
    for at, (i, k) in enumerate(units):
        if at + 1 < len(units):
            scores[(at + 1) % 2] = score(units[at + 1])
        u = scale * scores[at % 2] + shift
        if home and i == 0:
            text_row = lax.broadcasted_iota(jnp.int32, (SUB, rows), 0) + k
            diagonal = text_row == lax.broadcasted_iota(jnp.int32, (SUB, rows), 1)
            u = jnp.where(diagonal, -u, u)
        loss, slope = softplus_and_slope(u)
        coef = slope * (scale * flags[i])
        if home and i == 0:
            coef = jnp.where(diagonal, -coef, coef)
        coefs[i][k : k + SUB, :] = coef.astype(jnp.bfloat16)
        sums[i] = sums[i] + jnp.sum(loss.reshape(SUB // 8, 8, rows), axis=0)
        part = lax.dot_general(
            coefs[i][k : k + SUB, :],
            texts[i][k : k + SUB, :],
            (((0,), (0,)), ((), ())),
            preferred_element_type=jnp.float32,
        )
        if at == 0:
            total[...] = earlier[...] + part if add_to else part
        elif at + 1 < len(units):
            total[...] += part
        else:
            grad[...] = (total[...] + part).astype(grad.dtype)
    for i in range(blocks):
        losses[i] = jnp.sum(sums[i])


def tiles(scalars, flags, images, texts, home=False, earlier=None, grad_dtype=jnp.float32):
    blocks = len(texts)
    rows, width = images.shape
    text_rows = sum(t.shape[0] for t in texts)
    vmem = pl.BlockSpec(memory_space=pltpu.VMEM)
    smem = pl.BlockSpec(memory_space=pltpu.SMEM)
    add_to = earlier is not None
    extra = [earlier] if add_to else []
    out = pl.pallas_call(
        functools.partial(tiles_kernel, blocks, home, add_to),
        out_shape=[jax.ShapeDtypeStruct((t.shape[0], rows), jnp.bfloat16) for t in texts]
        + [
            jax.ShapeDtypeStruct((rows, width), grad_dtype),
            jax.ShapeDtypeStruct((blocks,), jnp.float32),
        ],
        in_specs=[smem, smem, vmem] + [vmem] * (blocks + len(extra)),
        out_specs=[vmem] * (blocks + 1) + [smem],
        scratch_shapes=[
            pltpu.VMEM((2, SUB, rows), jnp.float32),
            pltpu.VMEM((rows, width), jnp.float32),
        ],
        compiler_params=pltpu.CompilerParams(vmem_limit_bytes=VMEM_BYTES),
        cost_estimate=pl.CostEstimate(
            flops=4 * rows * text_rows * width,
            bytes_accessed=2 * (rows + text_rows) * width + 2 * rows * text_rows + 4 * rows * width,
            transcendentals=3 * rows * text_rows,
        ),
    )(scalars, flags, images, *texts, *extra)
    return out[:blocks], out[blocks], out[blocks + 1]


def text_kernel(pieces, halves, *refs):
    images = refs[:pieces]
    coefs = refs[pieces : pieces + pieces * halves]
    out = refs[pieces + pieces * halves]
    at = 0
    for h in range(halves):
        size = coefs[h * pieces].shape[0]
        part = None
        for p in range(pieces):
            one = jnp.dot(
                coefs[h * pieces + p][...], images[p][...], preferred_element_type=jnp.float32
            )
            part = one if part is None else part + one
        out[at : at + size, :] = part.astype(out.dtype)
        at += size


def text_partial(images, coefs, dtype):
    pieces, halves = len(images), len(coefs)
    width = images[0].shape[1]
    text_rows = sum(c[0].shape[0] for c in coefs)
    image_rows = sum(i.shape[0] for i in images)
    vmem = pl.BlockSpec(memory_space=pltpu.VMEM)
    flat = [c for run in coefs for c in run]
    return pl.pallas_call(
        functools.partial(text_kernel, pieces, halves),
        out_shape=jax.ShapeDtypeStruct((text_rows, width), dtype),
        in_specs=[vmem] * (pieces + len(flat)),
        out_specs=vmem,
        compiler_params=pltpu.CompilerParams(vmem_limit_bytes=VMEM_BYTES),
        cost_estimate=pl.CostEstimate(
            flops=2 * image_rows * text_rows * width,
            bytes_accessed=2 * image_rows * (text_rows + width) + 4 * text_rows * width,
            transcendentals=0,
        ),
    )(*images, *flat)


def shards(image_embeds, text_embeds, logit_scale, logit_bias, plan):
    pair_rows = image_embeds.shape[0]
    half = pair_rows // 2
    my_index = lax.axis_index("dp")
    round_masks = jnp.right_shift(jnp.bitwise_xor(plan[0], my_index), Z_BIT)
    scalars = jnp.concatenate([logit_scale, logit_bias])

    my_x = my_index >> X_SHIFT
    hops = jnp.array([0, 1, 3, 2, 2], jnp.int32)
    own_masks = ((my_x + hops) & 3 ^ my_x) << 1
    met = lambda masks: jnp.any(round_masks[None, :] == masks[:, None], axis=1)
    own_flags = jnp.where(met(own_masks) | (own_masks == 0), 1.0, 0.0).astype(jnp.float32)
    far_masks = own_masks | 1
    far_flags = jnp.where(met(far_masks), 1.0, 0.0).astype(jnp.float32)

    far_images = [to_z(image_embeds[:half]), to_z(image_embeds[half:])]
    text_below = to_x(text_embeds, 1)
    text_above = to_x(text_embeds, -1)
    text_across = [to_x(text_below[:half], 1), to_x(text_above[half:], -1)]
    near_texts = [text_embeds, text_above, text_below]
    all_texts = near_texts + text_across

    near_coefs, grad_near, loss_near = tiles(
        scalars, own_flags[:3], image_embeds, near_texts, home=True
    )
    far = [
        tiles(scalars, far_flags, images, all_texts, grad_dtype=jnp.bfloat16)
        for images in far_images
    ]
    returned = [to_z(grad) for _, grad, _ in far]
    far_loss = to_z(far[0][2] + far[1][2])
    across_coefs, grad_own, loss_across = tiles(
        scalars, own_flags[3:], image_embeds, text_across, earlier=grad_near
    )

    own_coefs = list(near_coefs) + list(across_coefs)
    images = [image_embeds] + far_images
    runs = [[own_coefs[i], far[0][0][i], far[1][0][i]] for i in range(5)]
    part_across = to_x(text_partial(images, runs[3:], jnp.bfloat16), 2)
    part_above = to_x(text_partial(images, runs[1:2], jnp.bfloat16), 1)
    part_below = to_x(text_partial(images, runs[2:3], jnp.bfloat16), -1)
    text_grad = text_partial(images, runs[:1], jnp.float32)

    text_grad = (
        text_grad
        + part_across.astype(jnp.float32)
        + part_above.astype(jnp.float32)
        + part_below.astype(jnp.float32)
    )
    image_grad = grad_own + jnp.concatenate(returned).astype(jnp.float32)

    sums = jnp.concatenate([loss_near, loss_across, far_loss])
    masks = jnp.concatenate([own_masks, far_masks])
    wanted = jnp.concatenate([jnp.zeros((1,), jnp.int32), round_masks])
    losses = jnp.sum(jnp.where(wanted[:, None] == masks[None, :], sums[None, :], 0.0), axis=1)
    losses = losses / (pair_rows * pair_rows)
    return (image_grad, text_grad, losses[None, :])


def solution(mesh):
    return jax.shard_map(
        shards,
        mesh=mesh,
        in_specs=(P("dp", None), P("dp", None), P(), P(), P("dp", None)),
        out_specs=(P("dp", None), P("dp", None), P("dp", None)),
        check_vma=False,
    )
```

```python
import functools

import jax
import jax.numpy as jnp
from jax import lax
from jax.experimental import pallas as pl
from jax.experimental.pallas import tpu as pltpu
from jax.sharding import PartitionSpec as P

X_SHIFT = 6
Z_BIT = 5
SUB = 256
FIRST = 256
VMEM_BYTES = 16 << 20
SMALL = pl.CostEstimate(flops=1024, bytes_accessed=1024, transcendentals=0)
MIDDLE = pl.CostEstimate(flops=1 << 31, bytes_accessed=1 << 20, transcendentals=0)
LARGE = pl.CostEstimate(flops=1 << 34, bytes_accessed=1 << 20, transcendentals=0)

ANY = pl.BlockSpec(memory_space=pl.ANY)
VMEM = pl.BlockSpec(memory_space=pltpu.VMEM)
SMEM = pl.BlockSpec(memory_space=pltpu.SMEM)


def x_neighbour(index, hop):
    x = index >> X_SHIFT
    return (index & ((1 << X_SHIFT) - 1)) | (((x + hop) & 3) << X_SHIFT)


def to_x(value, hop):
    count = lax.axis_size("dp")
    return lax.ppermute(value, "dp", [(i, x_neighbour(i, hop)) for i in range(count)])


def to_z(value):
    count = lax.axis_size("dp")
    return lax.ppermute(value, "dp", [(i, i ^ (1 << Z_BIT)) for i in range(count)])


def stage_kernel(starts, *refs):
    count = len(starts)
    sources, targets, sems = refs[:count], refs[-1 - count : -1], refs[-1]
    copies = [
        pltpu.make_async_copy(
            sources[i].at[pl.ds(starts[i], targets[i].shape[0]), :], targets[i], sems.at[i]
        )
        for i in range(count)
    ]
    for copy in copies:
        copy.start()
    for copy in copies:
        copy.wait()


def staged(parts):
    count = len(parts)
    return pl.pallas_call(
        functools.partial(stage_kernel, [first for _, first, _ in parts]),
        out_shape=[
            jax.ShapeDtypeStruct((rows, value.shape[1]), value.dtype) for value, _, rows in parts
        ],
        in_specs=[ANY] * count,
        out_specs=[VMEM] * count,
        scratch_shapes=[pltpu.SemaphoreType.DMA((count,))],
        compiler_params=pltpu.CompilerParams(vmem_limit_bytes=60 << 20),
        cost_estimate=SMALL,
    )(*[value for value, _, _ in parts])


def softplus_and_slope(u):
    decay = jnp.exp(-jnp.abs(u))
    ratio = 1.0 / (1.0 + decay)
    slope = jnp.where(u >= 0.0, ratio, decay * ratio)
    return jnp.maximum(u, 0.0) + jnp.log1p(decay), slope


def rows_by_rows(left, right):
    return lax.dot_general(
        left, right, (((1,), (1,)), ((), ())), preferred_element_type=jnp.float32
    )


def columns_by_columns(left, right):
    return lax.dot_general(
        left, right, (((0,), (0,)), ((), ())), preferred_element_type=jnp.float32
    )


def units_of(texts):
    return [(i, k) for i in range(len(texts)) for k in range(0, texts[i].shape[0], SUB)]


def tiles_kernel(blocks, home, add_to, with_grad, scalars, flags, after, images, *rest):
    texts = rest[:blocks]
    rest = rest[blocks:]
    if add_to:
        earlier, rest = rest[0], rest[1:]
    coefs, rest = rest[:blocks], rest[blocks:]
    if with_grad:
        grad, losses, scores, total = rest
    else:
        losses, scores = rest
    rows = images.shape[0]
    scale, shift = scalars[0], scalars[1]
    units = units_of(texts)

    def score(unit):
        i, k = unit
        return rows_by_rows(texts[i][k : k + SUB, :], images[...])

    sums = [jnp.zeros((8, rows), jnp.float32) for _ in range(blocks)]
    scores[0] = score(units[0])
    for at, (i, k) in enumerate(units):
        if at + 1 < len(units):
            scores[(at + 1) % 2] = score(units[at + 1])
        u = scale * scores[at % 2] + shift
        if home and i == 0:
            text_row = lax.broadcasted_iota(jnp.int32, (SUB, rows), 0) + k
            diagonal = text_row == lax.broadcasted_iota(jnp.int32, (SUB, rows), 1)
            u = jnp.where(diagonal, -u, u)
        loss, slope = softplus_and_slope(u)
        coef = slope * (scale * flags[i])
        if home and i == 0:
            coef = jnp.where(diagonal, -coef, coef)
        coefs[i][k : k + SUB, :] = coef.astype(jnp.bfloat16)
        sums[i] = sums[i] + jnp.sum(loss.reshape(SUB // 8, 8, rows), axis=0)
        if with_grad:
            part = columns_by_columns(coefs[i][k : k + SUB, :], texts[i][k : k + SUB, :])
            if at == 0:
                total[...] = earlier[...] + part if add_to else part
            elif at + 1 < len(units):
                total[...] += part
            else:
                grad[...] = (total[...] + part).astype(grad.dtype)
    for i in range(blocks):
        losses[i] = jnp.sum(sums[i])


def tiles(
    scalars, flags, after, images, texts, home=False, earlier=None, grad_dtype=jnp.float32
):
    blocks = len(texts)
    rows, width = images.shape
    extra = [] if earlier is None else [earlier]
    with_grad = grad_dtype is not None
    grad = [jax.ShapeDtypeStruct((rows, width), grad_dtype)] if with_grad else []
    total = [pltpu.VMEM((rows, width), jnp.float32)] if with_grad else []
    out = pl.pallas_call(
        functools.partial(tiles_kernel, blocks, home, len(extra) > 0, with_grad),
        out_shape=[jax.ShapeDtypeStruct((t.shape[0], rows), jnp.bfloat16) for t in texts]
        + grad
        + [jax.ShapeDtypeStruct((blocks,), jnp.float32)],
        in_specs=[SMEM, SMEM, SMEM, VMEM] + [VMEM] * (blocks + len(extra)),
        out_specs=[VMEM] * (blocks + len(grad)) + [SMEM],
        scratch_shapes=[pltpu.VMEM((2, SUB, rows), jnp.float32)] + total,
        compiler_params=pltpu.CompilerParams(vmem_limit_bytes=VMEM_BYTES),
        cost_estimate=SMALL,
    )(scalars, flags, after, images, *texts, *extra)
    return list(out[:blocks]), out[blocks], out[-1]


def image_grad_kernel(blocks, *refs):
    texts, coefs = refs[:blocks], refs[blocks : 2 * blocks]
    first_losses, second_losses = refs[2 * blocks : 2 * blocks + 2]
    grad, losses, total = refs[-3:]
    for i in range(blocks):
        losses[i] = first_losses[i] + second_losses[i]
    for i in range(blocks):
        part = columns_by_columns(coefs[i][...], texts[i][...])
        if i == 0:
            total[...] = part
        elif i + 1 < blocks:
            total[...] += part
        else:
            grad[...] = (total[...] + part).astype(grad.dtype)


def image_partial(texts, coefs, losses, after):
    blocks = len(texts)
    rows, width = coefs[0].shape[1], texts[0].shape[1]
    return pl.pallas_call(
        functools.partial(image_grad_kernel, blocks),
        out_shape=[
            jax.ShapeDtypeStruct((rows, width), jnp.bfloat16),
            jax.ShapeDtypeStruct((blocks,), jnp.float32),
        ],
        in_specs=[VMEM] * (2 * blocks) + [SMEM] * 2 + [ANY] * len(after),
        out_specs=[VMEM, SMEM],
        scratch_shapes=[pltpu.VMEM((rows, width), jnp.float32)],
        compiler_params=pltpu.CompilerParams(vmem_limit_bytes=VMEM_BYTES),
        cost_estimate=SMALL,
    )(*texts, *coefs, *losses, *after)


def text_kernel(pieces, runs, added, passed, *refs):
    images = refs[:pieces]
    coefs = refs[pieces : pieces + pieces * len(runs)]
    earlier = refs[pieces + pieces * len(runs) :][:added]
    outs = refs[len(refs) - len(runs) - passed :]
    if passed:
        given = refs[pieces + pieces * len(runs) + added]
        for i in range(given.shape[0]):
            outs[-1][i] = given[i]
    for r, (first, rows) in enumerate(runs):
        part = None
        for p in range(pieces):
            one = jnp.dot(
                coefs[r * pieces + p][first : first + rows, :],
                images[p][...],
                preferred_element_type=jnp.float32,
            )
            part = one if part is None else part + one
        if added:
            part = part + earlier[r][...].astype(jnp.float32)
        outs[r][...] = part.astype(outs[r].dtype)


def text_partials(images, runs, dtype, earlier=(), passed=(), after=(), cost=SMALL):
    width = images[0].shape[1]
    flat = [c for coefs, _, _ in runs for c in coefs]
    return pl.pallas_call(
        functools.partial(
            text_kernel, len(images), [(first, rows) for _, first, rows in runs], len(earlier), len(passed)
        ),
        out_shape=[jax.ShapeDtypeStruct((rows, width), dtype) for _, _, rows in runs]
        + [jax.ShapeDtypeStruct(p.shape, p.dtype) for p in passed],
        in_specs=[VMEM] * (len(images) + len(flat) + len(earlier))
        + [SMEM] * len(passed)
        + [ANY] * len(after),
        out_specs=[VMEM] * len(runs) + [SMEM] * len(passed),
        compiler_params=pltpu.CompilerParams(vmem_limit_bytes=VMEM_BYTES),
        cost_estimate=cost,
    )(*images, *flat, *earlier, *passed, *after)


def add_kernel(base, block, *refs):
    out, token = refs[-2:]
    out[...] = base[...] + block[...].astype(jnp.float32)
    token[0] = 0.0


def add_rows(base, block, first, into=None, cost=SMALL):
    rows, width = block.shape
    step_rows = rows // 2
    offset = first // step_rows
    rest = [] if into is None else [into]
    return pl.pallas_call(
        add_kernel,
        grid=(2,),
        out_shape=[
            jax.ShapeDtypeStruct(base.shape, jnp.float32),
            jax.ShapeDtypeStruct((1,), jnp.float32),
        ],
        in_specs=[
            pl.BlockSpec((step_rows, width), lambda i: (i + offset, 0)),
            pl.BlockSpec((step_rows, width), lambda i: (i, 0)),
        ]
        + [ANY] * len(rest),
        out_specs=[pl.BlockSpec((step_rows, width), lambda i: (i + offset, 0)), SMEM],
        input_output_aliases={2: 0} if rest else {},
        compiler_params=pltpu.CompilerParams(vmem_limit_bytes=VMEM_BYTES),
        cost_estimate=cost,
    )(base, block, *rest)


def join_kernel(low, high, low_more, high_more, out):
    step = pl.program_id(0)

    @pl.when(step == 0)
    def _():
        out[...] = low[...] + low_more[...].astype(jnp.float32)

    @pl.when(step == 1)
    def _():
        out[...] = high[...] + high_more[...].astype(jnp.float32)


def joined(low, high, low_more, high_more):
    rows, width = low.shape
    return pl.pallas_call(
        join_kernel,
        grid=(2,),
        out_shape=jax.ShapeDtypeStruct((2 * rows, width), jnp.float32),
        in_specs=[VMEM] * 4,
        out_specs=pl.BlockSpec((rows, width), lambda i: (i, 0)),
        compiler_params=pltpu.CompilerParams(vmem_limit_bytes=VMEM_BYTES),
        cost_estimate=SMALL,
    )(low, high, low_more, high_more)


def shards(image_embeds, text_embeds, logit_scale, logit_bias, plan):
    pair_rows = image_embeds.shape[0]
    half = pair_rows // 2
    my_index = lax.axis_index("dp")
    round_masks = jnp.right_shift(jnp.bitwise_xor(plan[0], my_index), Z_BIT)
    scalars = jnp.concatenate([logit_scale, logit_bias])

    my_x = my_index >> X_SHIFT
    hops = jnp.array([0, 1, 3, 2, 2], jnp.int32)
    own_masks = ((my_x + hops) & 3 ^ my_x) << 1
    met = lambda masks: jnp.any(round_masks[None, :] == masks[:, None], axis=1)
    own_flags = jnp.where(met(own_masks) | (own_masks == 0), 1.0, 0.0).astype(jnp.float32)
    far_masks = own_masks | 1
    far_flags = jnp.where(met(far_masks), 1.0, 0.0).astype(jnp.float32)

    far_images = [
        to_z(rows)
        for rows in staged(
            [(image_embeds, 0, FIRST), (image_embeds, FIRST, pair_rows - FIRST)]
        )
    ]
    text_below = to_x(text_embeds, 1)
    text_above = to_x(text_embeds, -1)
    text_across = [to_x(text_below[:half], 1), to_x(text_above[half:], -1)]
    near_texts = [text_embeds, text_above, text_below]
    all_texts = near_texts + text_across

    near_coefs, grad_near, loss_near = tiles(
        scalars, own_flags[:3], scalars, image_embeds, near_texts, home=True
    )
    first_coefs, first_grad, first_loss = tiles(
        scalars, far_flags, loss_near, far_images[0], all_texts, grad_dtype=jnp.bfloat16
    )
    across_coefs, grad_own, loss_across = tiles(
        scalars, own_flags[3:], first_loss, image_embeds, text_across, earlier=grad_near
    )
    second_coefs, _, second_loss = tiles(
        scalars, far_flags, loss_across, far_images[1], all_texts, grad_dtype=None
    )

    own_coefs = near_coefs + across_coefs
    images = [image_embeds] + far_images
    coefs = [[own_coefs[i], first_coefs[i], second_coefs[i]] for i in range(5)]
    across_low, across_high = text_partials(
        images, [(coefs[3], 0, half), (coefs[4], 0, half)], jnp.bfloat16
    )
    passing_low, passing_high = to_x(across_low, 1), to_x(across_high, -1)
    above_high, below_low = text_partials(
        images, [(coefs[1], half, half), (coefs[2], 0, half)], jnp.bfloat16, after=[across_low]
    )
    from_below_high, from_above_low = to_x(above_high, 1), to_x(below_low, -1)
    second_grad, far_loss = image_partial(
        all_texts, second_coefs, [first_loss, second_loss], [above_high]
    )
    returned = [to_z(first_grad), to_z(second_grad)]
    far_loss = to_z(far_loss)
    image_grad, token = add_rows(grad_own, returned[0], 0, cost=MIDDLE)
    above_low, below_high = text_partials(
        images,
        [(coefs[1], 0, half), (coefs[2], half, half)],
        jnp.bfloat16,
        earlier=[passing_low, passing_high],
        after=[token],
    )
    from_below_low, from_above_high = to_x(above_low, 1), to_x(below_high, -1)
    text_low, text_high, far_loss = text_partials(
        images,
        [(coefs[0], 0, half), (coefs[0], half, half)],
        jnp.float32,
        earlier=[from_above_low, from_below_high],
        passed=[far_loss],
        after=[above_low],
        cost=LARGE,
    )
    text_grad = joined(text_low, text_high, from_below_low, from_above_high)
    image_grad, _ = add_rows(grad_own, returned[1], FIRST, into=image_grad)

    sums = jnp.concatenate([loss_near, loss_across, far_loss])
    masks = jnp.concatenate([own_masks, far_masks])
    wanted = jnp.concatenate([jnp.zeros((1,), jnp.int32), round_masks])
    losses = jnp.sum(jnp.where(wanted[:, None] == masks[None, :], sums[None, :], 0.0), axis=1)
    losses = losses / (pair_rows * pair_rows)
    return (image_grad, text_grad, losses[None, :])


def solution(mesh):
    return jax.shard_map(
        shards,
        mesh=mesh,
        in_specs=(P("dp", None), P("dp", None), P(), P(), P("dp", None)),
        out_specs=(P("dp", None), P("dp", None), P("dp", None)),
        check_vma=False,
    )
```

```python
import functools

import jax
import jax.numpy as jnp
from jax import lax
from jax.experimental import pallas as pl
from jax.experimental.pallas import tpu as pltpu
from jax.sharding import PartitionSpec as P

X_SHIFT = 6
Z_BIT = 5
SUB = 256
FIRST = 256
VMEM_BYTES = 16 << 20
SMALL = pl.CostEstimate(flops=1024, bytes_accessed=1024, transcendentals=0)
MIDDLE = pl.CostEstimate(flops=1 << 31, bytes_accessed=1 << 20, transcendentals=0)
LARGE = pl.CostEstimate(flops=1 << 34, bytes_accessed=1 << 20, transcendentals=0)

ANY = pl.BlockSpec(memory_space=pl.ANY)
VMEM = pl.BlockSpec(memory_space=pltpu.VMEM)
SMEM = pl.BlockSpec(memory_space=pltpu.SMEM)


def x_neighbour(index, hop):
    x = index >> X_SHIFT
    return (index & ((1 << X_SHIFT) - 1)) | (((x + hop) & 3) << X_SHIFT)


def to_x(value, hop):
    count = lax.axis_size("dp")
    return lax.ppermute(value, "dp", [(i, x_neighbour(i, hop)) for i in range(count)])


def to_z(value):
    count = lax.axis_size("dp")
    return lax.ppermute(value, "dp", [(i, i ^ (1 << Z_BIT)) for i in range(count)])


def stage_kernel(starts, *refs):
    count = len(starts)
    sources, targets, sems = refs[:count], refs[-1 - count : -1], refs[-1]
    copies = [
        pltpu.make_async_copy(
            sources[i].at[pl.ds(starts[i], targets[i].shape[0]), :], targets[i], sems.at[i]
        )
        for i in range(count)
    ]
    for copy in copies:
        copy.start()
    for copy in copies:
        copy.wait()


def staged(parts):
    count = len(parts)
    return pl.pallas_call(
        functools.partial(stage_kernel, [first for _, first, _ in parts]),
        out_shape=[
            jax.ShapeDtypeStruct((rows, value.shape[1]), value.dtype) for value, _, rows in parts
        ],
        in_specs=[ANY] * count,
        out_specs=[VMEM] * count,
        scratch_shapes=[pltpu.SemaphoreType.DMA((count,))],
        compiler_params=pltpu.CompilerParams(vmem_limit_bytes=60 << 20),
        cost_estimate=SMALL,
    )(*[value for value, _, _ in parts])


def softplus_and_slope(u):
    decay = jnp.exp(-jnp.abs(u))
    ratio = 1.0 / (1.0 + decay)
    slope = jnp.where(u >= 0.0, ratio, decay * ratio)
    return jnp.maximum(u, 0.0) + jnp.log1p(decay), slope


def rows_by_rows(left, right):
    return lax.dot_general(
        left, right, (((1,), (1,)), ((), ())), preferred_element_type=jnp.float32
    )


def columns_by_columns(left, right):
    return lax.dot_general(
        left, right, (((0,), (0,)), ((), ())), preferred_element_type=jnp.float32
    )


def units_of(texts):
    return [(i, k) for i in range(len(texts)) for k in range(0, texts[i].shape[0], SUB)]


def tiles_kernel(blocks, home, add_to, with_grad, scalars, flags, after, images, *rest):
    texts = rest[:blocks]
    rest = rest[blocks:]
    if add_to:
        earlier, rest = rest[0], rest[1:]
    coefs, rest = rest[:blocks], rest[blocks:]
    if with_grad:
        grad, losses, scores, total = rest
    else:
        losses, scores = rest
    rows = images.shape[0]
    scale, shift = scalars[0], scalars[1]
    units = units_of(texts)

    def score(unit):
        i, k = unit
        return rows_by_rows(texts[i][k : k + SUB, :], images[...])

    sums = [jnp.zeros((8, rows), jnp.float32) for _ in range(blocks)]
    scores[0] = score(units[0])
    for at, (i, k) in enumerate(units):
        if at + 1 < len(units):
            scores[(at + 1) % 2] = score(units[at + 1])
        u = scale * scores[at % 2] + shift
        if home and i == 0:
            text_row = lax.broadcasted_iota(jnp.int32, (SUB, rows), 0) + k
            diagonal = text_row == lax.broadcasted_iota(jnp.int32, (SUB, rows), 1)
            u = jnp.where(diagonal, -u, u)
        loss, slope = softplus_and_slope(u)
        coef = slope * (scale * flags[i])
        if home and i == 0:
            coef = jnp.where(diagonal, -coef, coef)
        coefs[i][k : k + SUB, :] = coef.astype(jnp.bfloat16)
        sums[i] = sums[i] + jnp.sum(loss.reshape(SUB // 8, 8, rows), axis=0)
        if with_grad:
            part = columns_by_columns(coefs[i][k : k + SUB, :], texts[i][k : k + SUB, :])
            if at == 0:
                total[...] = earlier[...] + part if add_to else part
            elif at + 1 < len(units):
                total[...] += part
            else:
                grad[...] = (total[...] + part).astype(grad.dtype)
    for i in range(blocks):
        losses[i] = jnp.sum(sums[i])


def tiles(
    scalars, flags, after, images, texts, home=False, earlier=None, grad_dtype=jnp.float32
):
    blocks = len(texts)
    rows, width = images.shape
    extra = [] if earlier is None else [earlier]
    with_grad = grad_dtype is not None
    grad = [jax.ShapeDtypeStruct((rows, width), grad_dtype)] if with_grad else []
    total = [pltpu.VMEM((rows, width), jnp.float32)] if with_grad else []
    out = pl.pallas_call(
        functools.partial(tiles_kernel, blocks, home, len(extra) > 0, with_grad),
        out_shape=[jax.ShapeDtypeStruct((t.shape[0], rows), jnp.bfloat16) for t in texts]
        + grad
        + [jax.ShapeDtypeStruct((blocks,), jnp.float32)],
        in_specs=[SMEM, SMEM, SMEM, VMEM] + [VMEM] * (blocks + len(extra)),
        out_specs=[VMEM] * (blocks + len(grad)) + [SMEM],
        scratch_shapes=[pltpu.VMEM((2, SUB, rows), jnp.float32)] + total,
        compiler_params=pltpu.CompilerParams(vmem_limit_bytes=VMEM_BYTES),
        cost_estimate=SMALL,
    )(scalars, flags, after, images, *texts, *extra)
    return list(out[:blocks]), out[blocks], out[-1]


def image_grad_kernel(blocks, *refs):
    texts, coefs = refs[:blocks], refs[blocks : 2 * blocks]
    first_losses, second_losses = refs[2 * blocks : 2 * blocks + 2]
    grad, losses, total = refs[-3:]
    for i in range(blocks):
        losses[i] = first_losses[i] + second_losses[i]
    for i in range(blocks):
        part = columns_by_columns(coefs[i][...], texts[i][...])
        if i == 0:
            total[...] = part
        elif i + 1 < blocks:
            total[...] += part
        else:
            grad[...] = (total[...] + part).astype(grad.dtype)


def image_partial(texts, coefs, losses, after):
    blocks = len(texts)
    rows, width = coefs[0].shape[1], texts[0].shape[1]
    return pl.pallas_call(
        functools.partial(image_grad_kernel, blocks),
        out_shape=[
            jax.ShapeDtypeStruct((rows, width), jnp.bfloat16),
            jax.ShapeDtypeStruct((blocks,), jnp.float32),
        ],
        in_specs=[VMEM] * (2 * blocks) + [SMEM] * 2 + [ANY] * len(after),
        out_specs=[VMEM, SMEM],
        scratch_shapes=[pltpu.VMEM((rows, width), jnp.float32)],
        compiler_params=pltpu.CompilerParams(vmem_limit_bytes=VMEM_BYTES),
        cost_estimate=SMALL,
    )(*texts, *coefs, *losses, *after)


def text_kernel(pieces, runs, added, passed, *refs):
    images = refs[:pieces]
    coefs = refs[pieces : pieces + pieces * len(runs)]
    earlier = refs[pieces + pieces * len(runs) :][:added]
    outs = refs[len(refs) - len(runs) - passed :]
    if passed:
        given = refs[pieces + pieces * len(runs) + added]
        for i in range(given.shape[0]):
            outs[-1][i] = given[i]
    for r, (first, rows) in enumerate(runs):
        part = None
        for p in range(pieces):
            one = jnp.dot(
                coefs[r * pieces + p][first : first + rows, :],
                images[p][...],
                preferred_element_type=jnp.float32,
            )
            part = one if part is None else part + one
        if added:
            part = part + earlier[r][...].astype(jnp.float32)
        outs[r][...] = part.astype(outs[r].dtype)


def text_partials(images, runs, dtype, earlier=(), passed=(), after=(), cost=SMALL):
    width = images[0].shape[1]
    flat = [c for coefs, _, _ in runs for c in coefs]
    return pl.pallas_call(
        functools.partial(
            text_kernel, len(images), [(first, rows) for _, first, rows in runs], len(earlier), len(passed)
        ),
        out_shape=[jax.ShapeDtypeStruct((rows, width), dtype) for _, _, rows in runs]
        + [jax.ShapeDtypeStruct(p.shape, p.dtype) for p in passed],
        in_specs=[VMEM] * (len(images) + len(flat) + len(earlier))
        + [SMEM] * len(passed)
        + [ANY] * len(after),
        out_specs=[VMEM] * len(runs) + [SMEM] * len(passed),
        compiler_params=pltpu.CompilerParams(vmem_limit_bytes=VMEM_BYTES),
        cost_estimate=cost,
    )(*images, *flat, *earlier, *passed, *after)


def add_kernel(base, block, *refs):
    out, token = refs[-2:]
    out[...] = base[...] + block[...].astype(jnp.float32)
    token[0] = 0.0


def add_rows(base, block, first, into=None, cost=SMALL):
    rows, width = block.shape
    step_rows = rows // 2
    offset = first // step_rows
    rest = [] if into is None else [into]
    return pl.pallas_call(
        add_kernel,
        grid=(2,),
        out_shape=[
            jax.ShapeDtypeStruct(base.shape, jnp.float32),
            jax.ShapeDtypeStruct((1,), jnp.float32),
        ],
        in_specs=[
            pl.BlockSpec((step_rows, width), lambda i: (i + offset, 0)),
            pl.BlockSpec((step_rows, width), lambda i: (i, 0)),
        ]
        + [ANY] * len(rest),
        out_specs=[pl.BlockSpec((step_rows, width), lambda i: (i + offset, 0)), SMEM],
        input_output_aliases={2: 0} if rest else {},
        compiler_params=pltpu.CompilerParams(vmem_limit_bytes=VMEM_BYTES),
        cost_estimate=cost,
    )(base, block, *rest)


def join_kernel(low, high, low_more, high_more, out):
    step = pl.program_id(0)

    @pl.when(step == 0)
    def _():
        out[...] = low[...] + low_more[...].astype(jnp.float32)

    @pl.when(step == 1)
    def _():
        out[...] = high[...] + high_more[...].astype(jnp.float32)


def joined(low, high, low_more, high_more):
    rows, width = low.shape
    return pl.pallas_call(
        join_kernel,
        grid=(2,),
        out_shape=jax.ShapeDtypeStruct((2 * rows, width), jnp.float32),
        in_specs=[VMEM] * 4,
        out_specs=pl.BlockSpec((rows, width), lambda i: (i, 0)),
        compiler_params=pltpu.CompilerParams(vmem_limit_bytes=VMEM_BYTES),
        cost_estimate=SMALL,
    )(low, high, low_more, high_more)


def shards(image_embeds, text_embeds, logit_scale, logit_bias, plan):
    pair_rows = image_embeds.shape[0]
    half = pair_rows // 2
    my_index = lax.axis_index("dp")
    round_masks = jnp.right_shift(jnp.bitwise_xor(plan[0], my_index), Z_BIT)
    scalars = jnp.concatenate([logit_scale, logit_bias])

    my_x = my_index >> X_SHIFT
    hops = jnp.array([0, 1, 3, 2, 2], jnp.int32)
    own_masks = ((my_x + hops) & 3 ^ my_x) << 1
    met = lambda masks: jnp.any(round_masks[None, :] == masks[:, None], axis=1)
    own_flags = jnp.where(met(own_masks) | (own_masks == 0), 1.0, 0.0).astype(jnp.float32)
    far_masks = own_masks | 1
    far_flags = jnp.where(met(far_masks), 1.0, 0.0).astype(jnp.float32)

    far_images = [
        to_z(rows)
        for rows in staged(
            [(image_embeds, 0, FIRST), (image_embeds, FIRST, pair_rows - FIRST)]
        )
    ]
    text_below = to_x(text_embeds, 1)
    text_above = to_x(text_embeds, -1)
    text_across = [to_x(text_below[:half], 1), to_x(text_above[half:], -1)]
    near_texts = [text_embeds, text_above, text_below]
    all_texts = near_texts + text_across

    near_coefs, grad_near, loss_near = tiles(
        scalars, own_flags[:3], scalars, image_embeds, near_texts, home=True
    )
    first_coefs, first_grad, first_loss = tiles(
        scalars, far_flags, loss_near, far_images[0], all_texts, grad_dtype=jnp.bfloat16
    )
    across_coefs, grad_own, loss_across = tiles(
        scalars, own_flags[3:], first_loss, image_embeds, text_across, earlier=grad_near
    )
    second_coefs, _, second_loss = tiles(
        scalars, far_flags, loss_across, far_images[1], all_texts, grad_dtype=None
    )

    own_coefs = near_coefs + across_coefs
    images = [image_embeds] + far_images
    coefs = [[own_coefs[i], first_coefs[i], second_coefs[i]] for i in range(5)]
    across_low, across_high = text_partials(
        images, [(coefs[3], 0, half), (coefs[4], 0, half)], jnp.bfloat16
    )
    passing_low, passing_high = to_x(across_low, 1), to_x(across_high, -1)
    above_high, below_low = text_partials(
        images, [(coefs[1], half, half), (coefs[2], 0, half)], jnp.bfloat16, after=[across_low]
    )
    from_below_high, from_above_low = to_x(above_high, 1), to_x(below_low, -1)
    second_grad, far_loss = image_partial(
        all_texts, second_coefs, [first_loss, second_loss], [above_high]
    )
    returned = [to_z(first_grad), to_z(second_grad)]
    far_loss = to_z(far_loss)
    image_grad, token = add_rows(grad_own, returned[0], 0, cost=MIDDLE)
    above_low, below_high = text_partials(
        images,
        [(coefs[1], 0, half), (coefs[2], half, half)],
        jnp.bfloat16,
        earlier=[passing_low, passing_high],
        after=[token],
    )
    from_below_low, from_above_high = to_x(above_low, 1), to_x(below_high, -1)
    text_low, text_high, far_loss = text_partials(
        images,
        [(coefs[0], 0, half), (coefs[0], half, half)],
        jnp.float32,
        earlier=[from_above_low, from_below_high],
        passed=[far_loss],
        after=[above_low],
        cost=LARGE,
    )
    text_grad = joined(text_low, text_high, from_below_low, from_above_high)
    grad_own, text_grad = lax.optimization_barrier((grad_own, text_grad))
    image_grad, _ = add_rows(grad_own, returned[1], FIRST, into=image_grad)

    sums = jnp.concatenate([loss_near, loss_across, far_loss])
    masks = jnp.concatenate([own_masks, far_masks])
    wanted = jnp.concatenate([jnp.zeros((1,), jnp.int32), round_masks])
    losses = jnp.sum(jnp.where(wanted[:, None] == masks[None, :], sums[None, :], 0.0), axis=1)
    losses = losses / (pair_rows * pair_rows)
    return (image_grad, text_grad, losses[None, :])


def solution(mesh):
    return jax.shard_map(
        shards,
        mesh=mesh,
        in_specs=(P("dp", None), P("dp", None), P(), P(), P("dp", None)),
        out_specs=(P("dp", None), P("dp", None), P("dp", None)),
        check_vma=False,
    )
```

```python
import functools

import jax
import jax.numpy as jnp
from jax import lax
from jax.experimental import pallas as pl
from jax.experimental.pallas import tpu as pltpu
from jax.sharding import PartitionSpec as P

X_SHIFT = 6
Z_BIT = 5
SUB = 256
FIRST = 256
VMEM_BYTES = 16 << 20
SMALL = pl.CostEstimate(flops=1024, bytes_accessed=1024, transcendentals=0)
MIDDLE = pl.CostEstimate(flops=1 << 31, bytes_accessed=1 << 20, transcendentals=0)
LARGE = pl.CostEstimate(flops=1 << 34, bytes_accessed=1 << 20, transcendentals=0)

ANY = pl.BlockSpec(memory_space=pl.ANY)
VMEM = pl.BlockSpec(memory_space=pltpu.VMEM)
SMEM = pl.BlockSpec(memory_space=pltpu.SMEM)


def x_neighbour(index, hop):
    x = index >> X_SHIFT
    return (index & ((1 << X_SHIFT) - 1)) | (((x + hop) & 3) << X_SHIFT)


def to_x(value, hop):
    count = lax.axis_size("dp")
    return lax.ppermute(value, "dp", [(i, x_neighbour(i, hop)) for i in range(count)])


def to_z(value):
    count = lax.axis_size("dp")
    return lax.ppermute(value, "dp", [(i, i ^ (1 << Z_BIT)) for i in range(count)])


def stage_kernel(value, *halves):
    first = 0
    for half in halves:
        half[...] = value[first : first + half.shape[0], :]
        first += half.shape[0]


def staged(value, rows):
    return pl.pallas_call(
        stage_kernel,
        out_shape=[jax.ShapeDtypeStruct((r, value.shape[1]), value.dtype) for r in rows],
        in_specs=[VMEM],
        out_specs=[VMEM] * len(rows),
        compiler_params=pltpu.CompilerParams(vmem_limit_bytes=8 << 20),
        cost_estimate=SMALL,
    )(value)


def softplus_and_slope(u):
    decay = jnp.exp(-jnp.abs(u))
    ratio = 1.0 / (1.0 + decay)
    slope = jnp.where(u >= 0.0, ratio, decay * ratio)
    return jnp.maximum(u, 0.0) + jnp.log1p(decay), slope


def rows_by_rows(left, right):
    return lax.dot_general(
        left, right, (((1,), (1,)), ((), ())), preferred_element_type=jnp.float32
    )


def columns_by_columns(left, right):
    return lax.dot_general(
        left, right, (((0,), (0,)), ((), ())), preferred_element_type=jnp.float32
    )


def units_of(texts):
    return [(i, k) for i in range(len(texts)) for k in range(0, texts[i].shape[0], SUB)]


def tiles_kernel(blocks, home, add_to, with_grad, scalars, flags, after, images, *rest):
    texts = rest[:blocks]
    rest = rest[blocks:]
    if add_to:
        earlier, rest = rest[0], rest[1:]
    coefs, rest = rest[:blocks], rest[blocks:]
    if with_grad:
        grad, losses, scores, total = rest
    else:
        losses, scores = rest
    rows = images.shape[0]
    scale, shift = scalars[0], scalars[1]
    units = units_of(texts)

    def score(unit):
        i, k = unit
        return rows_by_rows(texts[i][k : k + SUB, :], images[...])

    sums = [jnp.zeros((8, rows), jnp.float32) for _ in range(blocks)]
    scores[0] = score(units[0])
    for at, (i, k) in enumerate(units):
        if at + 1 < len(units):
            scores[(at + 1) % 2] = score(units[at + 1])
        u = scale * scores[at % 2] + shift
        if home and i == 0:
            text_row = lax.broadcasted_iota(jnp.int32, (SUB, rows), 0) + k
            diagonal = text_row == lax.broadcasted_iota(jnp.int32, (SUB, rows), 1)
            u = jnp.where(diagonal, -u, u)
        loss, slope = softplus_and_slope(u)
        coef = slope * (scale * flags[i])
        if home and i == 0:
            coef = jnp.where(diagonal, -coef, coef)
        coefs[i][k : k + SUB, :] = coef.astype(jnp.bfloat16)
        sums[i] = sums[i] + jnp.sum(loss.reshape(SUB // 8, 8, rows), axis=0)
        if with_grad:
            part = columns_by_columns(coefs[i][k : k + SUB, :], texts[i][k : k + SUB, :])
            if at == 0:
                total[...] = earlier[...] + part if add_to else part
            elif at + 1 < len(units):
                total[...] += part
            else:
                grad[...] = (total[...] + part).astype(grad.dtype)
    for i in range(blocks):
        losses[i] = jnp.sum(sums[i])


def tiles(
    scalars, flags, after, images, texts, home=False, earlier=None, grad_dtype=jnp.float32
):
    blocks = len(texts)
    rows, width = images.shape
    extra = [] if earlier is None else [earlier]
    with_grad = grad_dtype is not None
    grad = [jax.ShapeDtypeStruct((rows, width), grad_dtype)] if with_grad else []
    total = [pltpu.VMEM((rows, width), jnp.float32)] if with_grad else []
    out = pl.pallas_call(
        functools.partial(tiles_kernel, blocks, home, len(extra) > 0, with_grad),
        out_shape=[jax.ShapeDtypeStruct((t.shape[0], rows), jnp.bfloat16) for t in texts]
        + grad
        + [jax.ShapeDtypeStruct((blocks,), jnp.float32)],
        in_specs=[SMEM, SMEM, SMEM, VMEM] + [VMEM] * (blocks + len(extra)),
        out_specs=[VMEM] * (blocks + len(grad)) + [SMEM],
        scratch_shapes=[pltpu.VMEM((2, SUB, rows), jnp.float32)] + total,
        compiler_params=pltpu.CompilerParams(vmem_limit_bytes=VMEM_BYTES),
        cost_estimate=SMALL,
    )(scalars, flags, after, images, *texts, *extra)
    return list(out[:blocks]), out[blocks], out[-1]


def image_grad_kernel(blocks, *refs):
    texts, coefs = refs[:blocks], refs[blocks : 2 * blocks]
    first_losses, second_losses = refs[2 * blocks : 2 * blocks + 2]
    grad, losses, total = refs[-3:]
    for i in range(blocks):
        losses[i] = first_losses[i] + second_losses[i]
    for i in range(blocks):
        part = columns_by_columns(coefs[i][...], texts[i][...])
        if i == 0:
            total[...] = part
        elif i + 1 < blocks:
            total[...] += part
        else:
            grad[...] = (total[...] + part).astype(grad.dtype)


def image_partial(texts, coefs, losses, after):
    blocks = len(texts)
    rows, width = coefs[0].shape[1], texts[0].shape[1]
    return pl.pallas_call(
        functools.partial(image_grad_kernel, blocks),
        out_shape=[
            jax.ShapeDtypeStruct((rows, width), jnp.bfloat16),
            jax.ShapeDtypeStruct((blocks,), jnp.float32),
        ],
        in_specs=[VMEM] * (2 * blocks) + [SMEM] * 2 + [ANY] * len(after),
        out_specs=[VMEM, SMEM],
        scratch_shapes=[pltpu.VMEM((rows, width), jnp.float32)],
        compiler_params=pltpu.CompilerParams(vmem_limit_bytes=VMEM_BYTES),
        cost_estimate=SMALL,
    )(*texts, *coefs, *losses, *after)


def text_kernel(pieces, runs, added, passed, *refs):
    images = refs[:pieces]
    coefs = refs[pieces : pieces + pieces * len(runs)]
    earlier = refs[pieces + pieces * len(runs) :][:added]
    outs = refs[len(refs) - len(runs) - passed :]
    if passed:
        given = refs[pieces + pieces * len(runs) + added]
        for i in range(given.shape[0]):
            outs[-1][i] = given[i]
    for r, (first, rows) in enumerate(runs):
        part = None
        for p in range(pieces):
            one = jnp.dot(
                coefs[r * pieces + p][first : first + rows, :],
                images[p][...],
                preferred_element_type=jnp.float32,
            )
            part = one if part is None else part + one
        if added:
            part = part + earlier[r][...].astype(jnp.float32)
        outs[r][...] = part.astype(outs[r].dtype)


def text_partials(images, runs, dtype, earlier=(), passed=(), after=(), cost=SMALL):
    width = images[0].shape[1]
    flat = [c for coefs, _, _ in runs for c in coefs]
    return pl.pallas_call(
        functools.partial(
            text_kernel, len(images), [(first, rows) for _, first, rows in runs], len(earlier), len(passed)
        ),
        out_shape=[jax.ShapeDtypeStruct((rows, width), dtype) for _, _, rows in runs]
        + [jax.ShapeDtypeStruct(p.shape, p.dtype) for p in passed],
        in_specs=[VMEM] * (len(images) + len(flat) + len(earlier))
        + [SMEM] * len(passed)
        + [ANY] * len(after),
        out_specs=[VMEM] * len(runs) + [SMEM] * len(passed),
        compiler_params=pltpu.CompilerParams(vmem_limit_bytes=VMEM_BYTES),
        cost_estimate=cost,
    )(*images, *flat, *earlier, *passed, *after)


def add_kernel(base, block, *refs):
    out, token = refs[-2:]
    out[...] = base[...] + block[...].astype(jnp.float32)
    token[0] = 0.0


def add_rows(base, block, first, into=None, cost=SMALL):
    rows, width = block.shape
    step_rows = rows // 2
    offset = first // step_rows
    rest = [] if into is None else [into]
    return pl.pallas_call(
        add_kernel,
        grid=(2,),
        out_shape=[
            jax.ShapeDtypeStruct(base.shape, jnp.float32),
            jax.ShapeDtypeStruct((1,), jnp.float32),
        ],
        in_specs=[
            pl.BlockSpec((step_rows, width), lambda i: (i + offset, 0)),
            pl.BlockSpec((step_rows, width), lambda i: (i, 0)),
        ]
        + [ANY] * len(rest),
        out_specs=[pl.BlockSpec((step_rows, width), lambda i: (i + offset, 0)), SMEM],
        input_output_aliases={2: 0} if rest else {},
        compiler_params=pltpu.CompilerParams(vmem_limit_bytes=VMEM_BYTES),
        cost_estimate=cost,
    )(base, block, *rest)


def join_kernel(low, high, low_more, high_more, out):
    step = pl.program_id(0)

    @pl.when(step == 0)
    def _():
        out[...] = low[...] + low_more[...].astype(jnp.float32)

    @pl.when(step == 1)
    def _():
        out[...] = high[...] + high_more[...].astype(jnp.float32)


def joined(low, high, low_more, high_more):
    rows, width = low.shape
    return pl.pallas_call(
        join_kernel,
        grid=(2,),
        out_shape=jax.ShapeDtypeStruct((2 * rows, width), jnp.float32),
        in_specs=[VMEM] * 4,
        out_specs=pl.BlockSpec((rows, width), lambda i: (i, 0)),
        compiler_params=pltpu.CompilerParams(vmem_limit_bytes=VMEM_BYTES),
        cost_estimate=SMALL,
    )(low, high, low_more, high_more)


def shards(image_embeds, text_embeds, logit_scale, logit_bias, plan):
    pair_rows = image_embeds.shape[0]
    half = pair_rows // 2
    my_index = lax.axis_index("dp")
    round_masks = jnp.right_shift(jnp.bitwise_xor(plan[0], my_index), Z_BIT)
    scalars = jnp.concatenate([logit_scale, logit_bias])

    my_x = my_index >> X_SHIFT
    hops = jnp.array([0, 1, 3, 2, 2], jnp.int32)
    own_masks = ((my_x + hops) & 3 ^ my_x) << 1
    met = lambda masks: jnp.any(round_masks[None, :] == masks[:, None], axis=1)
    own_flags = jnp.where(met(own_masks) | (own_masks == 0), 1.0, 0.0).astype(jnp.float32)
    far_masks = own_masks | 1
    far_flags = jnp.where(met(far_masks), 1.0, 0.0).astype(jnp.float32)

    far_images = [
        to_z(rows)
        for rows in staged(image_embeds, [FIRST, pair_rows - FIRST])
    ]
    text_below = to_x(text_embeds, 1)
    text_above = to_x(text_embeds, -1)
    text_across = [to_x(text_below[:half], 1), to_x(text_above[half:], -1)]
    near_texts = [text_embeds, text_above, text_below]
    all_texts = near_texts + text_across

    near_coefs, grad_near, loss_near = tiles(
        scalars, own_flags[:3], scalars, image_embeds, near_texts, home=True
    )
    first_coefs, first_grad, first_loss = tiles(
        scalars, far_flags, loss_near, far_images[0], all_texts, grad_dtype=jnp.bfloat16
    )
    across_coefs, grad_own, loss_across = tiles(
        scalars, own_flags[3:], first_loss, image_embeds, text_across, earlier=grad_near
    )
    second_coefs, _, second_loss = tiles(
        scalars, far_flags, loss_across, far_images[1], all_texts, grad_dtype=None
    )

    own_coefs = near_coefs + across_coefs
    images = [image_embeds] + far_images
    coefs = [[own_coefs[i], first_coefs[i], second_coefs[i]] for i in range(5)]
    across_low, across_high = text_partials(
        images, [(coefs[3], 0, half), (coefs[4], 0, half)], jnp.bfloat16
    )
    passing_low, passing_high = to_x(across_low, 1), to_x(across_high, -1)
    above_high, below_low = text_partials(
        images, [(coefs[1], half, half), (coefs[2], 0, half)], jnp.bfloat16, after=[across_low]
    )
    from_below_high, from_above_low = to_x(above_high, 1), to_x(below_low, -1)
    second_grad, far_loss = image_partial(
        all_texts, second_coefs, [first_loss, second_loss], [above_high]
    )
    returned = [to_z(first_grad), to_z(second_grad)]
    far_loss = to_z(far_loss)
    image_grad, token = add_rows(grad_own, returned[0], 0, cost=MIDDLE)
    above_low, below_high = text_partials(
        images,
        [(coefs[1], 0, half), (coefs[2], half, half)],
        jnp.bfloat16,
        earlier=[passing_low, passing_high],
        after=[token],
    )
    from_below_low, from_above_high = to_x(above_low, 1), to_x(below_high, -1)
    text_low, text_high, far_loss = text_partials(
        images,
        [(coefs[0], 0, half), (coefs[0], half, half)],
        jnp.float32,
        earlier=[from_above_low, from_below_high],
        passed=[far_loss],
        after=[above_low],
        cost=LARGE,
    )
    text_grad = joined(text_low, text_high, from_below_low, from_above_high)
    grad_own, text_grad = lax.optimization_barrier((grad_own, text_grad))
    image_grad, _ = add_rows(grad_own, returned[1], FIRST, into=image_grad)

    sums = jnp.concatenate([loss_near, loss_across, far_loss])
    masks = jnp.concatenate([own_masks, far_masks])
    wanted = jnp.concatenate([jnp.zeros((1,), jnp.int32), round_masks])
    losses = jnp.sum(jnp.where(wanted[:, None] == masks[None, :], sums[None, :], 0.0), axis=1)
    losses = losses / (pair_rows * pair_rows)
    return (image_grad, text_grad, losses[None, :])


def solution(mesh):
    return jax.shard_map(
        shards,
        mesh=mesh,
        in_specs=(P("dp", None), P("dp", None), P(), P(), P("dp", None)),
        out_specs=(P("dp", None), P("dp", None), P("dp", None)),
        check_vma=False,
    )
```
